32 devices in a mesh: fields: 2 (over x), prow: 8 (over z, y), pcol: 2 (over core).
Axes of the slice: x: 2, y: 2, z: 4, core: 2. Of those that a mesh axis runs over, the one named last changes fastest.
Arguments:
- inverse_tiles: bfloat16 [32, 16, 256, 256], P(('fields', 'prow'), 'pcol'), parts along dimension 0, may hold values from -6 to 6
- panel_blocks: bfloat16 [4, 8, 256, 512], P('fields', 'prow', None, 'pcol'), parts along dimension 0, may hold values from -0.125 to 0.125
- diag_inverse: float32 [4, 512], P('fields', 'pcol'), parts along dimension 0, may hold values from 0.5 to 2
- structure: int32 [4, 8], P('fields'), parts along dimension 0, may hold values from 0 to 15, as said below
- block_slot: int32 [32], P('fields'), parts along dimension 0, may hold values from 0 to 15, each once
Outputs:
- sigma_new: bfloat16 [4, 16, 256, 512], P('fields', 'prow', None, 'pcol'), parts along dimension 0
- variances: float32 [4, 512], P('fields', 'pcol'), parts along dimension 0
The draws below stay inside these ranges and needn't reach their ends.
There are 2 independent parts, one for each index of `fields`. The reference program is written for one: setup_inputs(seed, part) draws one part's arguments, and reference() takes and returns one part's arrays. A program takes and returns all parts, laid end to end along the dimension named above; each array names one. Nothing has to cross between parts.
Inputs may be any that keep to these rules, and one draw needn't show every extreme that they name: `structure`: each row lists 8 distinct row blocks in increasing order, and the last is always 16 - 1. `block_slot`: each slot is used by exactly one row block.
All inputs are finite; a program needn't handle non-finite values.
Results may differ from the reference program's by a relative error of at most 0.0006.
Values may be sent and summed in bfloat16 or wider, within the bound.
A program may use at most 128 MiB of HBM per device.

```python
import math
import jax
import jax.numpy as jnp
from jax import lax

W = 512
B = 256
NSUP = 2
NB = 16
R = 8


def draw_structure(key, part):

    def single_list(subkey):
        order = jax.random.permutation(subkey, NB - 1).astype(jnp.int32)
        chosen = jnp.concatenate([order[:R - 1], jnp.full((1,), NB - 1, jnp.int32)])
        return jnp.sort(chosen)
    keys = jax.random.split(jax.random.fold_in(key, 7), NSUP)
    return jax.vmap(single_list)(keys)


def shard_levels(stream_key, extent, pieces, least, top_value):
    def one(axis_at, shards_of):
        draws = jax.random.uniform(jax.random.fold_in(jax.random.fold_in(stream_key, 6), axis_at), (shards_of,), jnp.float32, least / len(pieces), top_value / len(pieces))
        return jnp.repeat(jnp.exp(draws), extent[axis_at] // shards_of).reshape((-1,) + (1,) * (len(extent) - axis_at - 1))

    gain = one(*pieces[0])
    for cut in pieces[1:]:
        gain = gain * one(*cut)
    return gain


def centred(stream_key, extent, width, limit, cuts=(), kind=jnp.bfloat16):
    loudness = shard_levels(stream_key, extent, cuts, -0.22, 0.18) if cuts else 1.0
    values = jax.random.normal(stream_key, extent, jnp.float32) * width * loudness
    return jnp.minimum(jnp.maximum(values, -limit), limit).astype(kind)


def setup_inputs(seed: int = 0, part: int = 0) -> dict:
    arg_keys = jax.random.split(jax.random.key(seed), 6)
    part_splits = jax.random.split(jax.random.fold_in(arg_keys[5], part), 6)
    return {
        "inverse_tiles": centred(part_splits[0], (NB, NB, B, B), 1.0, 6.0, ((0, 8), (1, 2))),
        "panel_blocks": centred(part_splits[1], (NSUP, R, B, W), (R * B) ** -0.5, 0.125, ((1, 8), (3, 2))),
        "diag_inverse": jnp.clip(jnp.exp(math.log(2.0) - 1.3862944 * jax.random.uniform(part_splits[2], (NSUP, W), jnp.float32) ** shard_levels(part_splits[2], (NSUP, W), ((1, 2),), -0.2, 0.2)), 0.5, 2.0),
        "structure": draw_structure(jax.random.fold_in(jax.random.fold_in(arg_keys[5], part), 71), part),
        "block_slot": jax.random.permutation(part_splits[4], NB).astype(jnp.int32),
    }


def reference(inverse_tiles, panel_blocks, diag_inverse, structure, block_slot):
    sigma_list = []
    variance_list = []
    for sup_index in range(NSUP):
        slot_of = block_slot[structure[sup_index]].astype(jnp.int32)
        gathered = inverse_tiles[slot_of][:, slot_of].astype(jnp.float32)
        panel_full = panel_blocks[sup_index].astype(jnp.float32)
        sigma_rows = -jnp.einsum("abxy,byw->axw", gathered, panel_full, precision=lax.Precision.HIGHEST)
        stored = jnp.zeros((NB, B, W), jnp.bfloat16).at[slot_of].set(sigma_rows.astype(jnp.bfloat16))
        variance = diag_inverse[sup_index] - jnp.einsum("axw,axw->w", panel_full, sigma_rows, precision=lax.Precision.HIGHEST)
        sigma_list.append(stored)
        variance_list.append(variance)
    return jnp.stack(sigma_list), jnp.stack(variance_list)
```

```python
import functools

import jax
import jax.numpy as jnp
from jax import lax
from jax.experimental import pallas as pl
from jax.experimental.pallas import tpu as pltpu
from jax.sharding import PartitionSpec as P

MESH = pl.DeviceIdType.MESH
UP, DOWN, ACROSS, EXTRA = range(4)


def grid_of(mesh):
    count = mesh.shape["prow"]
    line = None
    devices = getattr(mesh, "devices", None)
    if devices is not None and hasattr(devices.flat[0], "coords"):
        line = len({tuple(d.coords)[2] for d in devices[0, :, 0]})
    if line is None and count % 2 == 0:
        line = count // 2
    if line is None or line * 2 != count or line % 2:
        return count, 1
    return line, 2


def kernel(
    line, wide, structure, block_slot, tiles, panel, diag, sigma, variance,
    full, acc, part, parts, *rest,
):
    supers = structure.shape[0]
    positions = structure.shape[1]
    rows, columns, tile = tiles.shape[0], tiles.shape[1], tiles.shape[2]
    width = panel.shape[3]
    held = positions // (line * wide)
    count = line * wide
    panels = rest[:supers]
    (
        panel_sem, send_sem, recv_sem, tile_sem, tile_send, tile_recv,
        part_send, part_recv,
    ) = rest[supers:]

    me = lax.axis_index("prow")
    core = lax.axis_index("pcol")
    z, y = me // wide, me % wide
    sibling = z * wide + (wide - 1 - y)
    twin = (z + 1 - 2 * (z % 2)) * wide + y
    last = supers - 1

    def at(zz, yy):
        return zz * wide + yy

    barrier = pltpu.get_barrier_semaphore()
    for shift in range(1, count):
        pl.semaphore_signal(
            barrier, inc=1, device_id={"prow": lax.rem(me + shift, count)},
            device_id_type=MESH,
        )
    pl.semaphore_signal(barrier, inc=1, device_id={"pcol": 1 - core}, device_id_type=MESH)
    pl.semaphore_wait(barrier, count)

    def send(s, source, kind, to, own=False):
        return pltpu.make_async_remote_copy(
            src_ref=panel.at[s] if own else panels[s].at[source],
            dst_ref=panels[s].at[source],
            send_sem=send_sem.at[kind, s, source],
            recv_sem=recv_sem.at[s, source],
            device_id={"prow": to},
            device_id_type=MESH,
        )

    def arrive(s, source):
        send(s, source, UP, me).wait_recv()

    up, down = at(z + 1, y), at(z - 1, y)
    has_up, has_down = z + 1 < line, z >= 1

    for s in range(supers):
        if wide == 2:
            send(s, me, ACROSS, sibling, True).start()

        @pl.when(has_up)
        def _():
            send(s, me, UP, up, True).start()

        @pl.when(has_down)
        def _():
            send(s, me, DOWN, down, True).start()

    swap = pltpu.make_async_remote_copy(
        src_ref=tiles,
        dst_ref=full.at[:, pl.ds(core * columns, columns)],
        send_sem=tile_send,
        recv_sem=tile_recv,
        device_id={"pcol": 1 - core},
        device_id_type=MESH,
    )
    swap.start()
    keep = pltpu.make_async_copy(
        tiles, full.at[:, pl.ds(core * columns, columns)], tile_sem
    )
    keep.start()
    own = [
        pltpu.make_async_copy(panel.at[s], panels[s].at[me], panel_sem.at[s])
        for s in range(supers)
    ]
    for s in range(supers):
        own[s].start()
    for s in range(supers):
        acc[s] = jnp.zeros(acc.shape[1:], acc.dtype)

    def add(s, source):
        for k in range(held):
            slot = block_slot[structure[s, source * held + k]]
            left = full[:, slot].reshape(rows * tile, tile)
            acc[s] += jnp.dot(
                left, panels[s][source, k], preferred_element_type=jnp.float32
            )

    def crosses(s, zz):
        if s != last:
            return zz >= 0
        return zz != z + 1 - 2 * (z % 2)

    def flush():
        for s in range(supers):
            own[s].wait()
        keep.wait()
        swap.wait_recv()
        for s in range(supers):
            add(s, me)

    def step(d, _):
        above, below = z + d, z - d
        for s in range(supers):
            @pl.when(above < line)
            def _():
                arrive(s, at(above, y))

                @pl.when(has_down)
                def _():
                    send(s, at(above, y), DOWN, down).start()

                if wide == 2:
                    @pl.when(crosses(s, above))
                    def _():
                        send(s, at(above, y), ACROSS, sibling).start()

            @pl.when(below >= 0)
            def _():
                arrive(s, at(below, y))

                @pl.when(has_up)
                def _():
                    send(s, at(below, y), UP, up).start()

                if wide == 2:
                    @pl.when(crosses(s, below))
                    def _():
                        send(s, at(below, y), ACROSS, sibling).start()

            if s == 0:
                @pl.when(d == 1)
                def _():
                    flush()

            @pl.when(above < line)
            def _():
                add(s, at(above, y))

            @pl.when(below >= 0)
            def _():
                add(s, at(below, y))

            if wide == 2:
                across(s, d - 1)
        return 0

    def across(s, d):
        above, below = z + d, z - d

        @pl.when((above < line) & crosses(s, above))
        def _():
            arrive(s, at(above, 1 - y))
            add(s, at(above, 1 - y))

        @pl.when((below >= 0) & crosses(s, below) & (d > 0))
        def _():
            arrive(s, at(below, 1 - y))
            add(s, at(below, 1 - y))

    lax.fori_loop(1, line, step, 0)

    if wide == 2:
        extra = send(last, sibling, EXTRA, twin)
        extra.start()

    def finish(s):
        total = jnp.zeros((1, width), jnp.float32)
        for r in range(rows):
            row = me * rows + r
            position, used = jnp.int32(0), jnp.int32(0)
            for a in range(positions):
                hit = block_slot[structure[s, a]] == row
                position = jnp.where(hit, a, position)
                used = jnp.where(hit, 1, used)
            value = jnp.where(used > 0, -acc[s, r * tile:(r + 1) * tile, :], 0.0)
            sigma[s, r] = value.astype(sigma.dtype)
            mine = panels[s][position // held, position % held].astype(jnp.float32)
            total = total + jnp.sum(mine * value, axis=0, keepdims=True)
        part[s:s + 1, :] = total

    for s in range(supers):
        if wide == 2:
            across(s, line - 1)
            if s == last:
                arrive(s, at(z + 1 - 2 * (z % 2), 1 - y))
                add(s, at(z + 1 - 2 * (z % 2), 1 - y))
        finish(s)

    def share(shift):
        to = lax.rem(me + shift, count)
        return pltpu.make_async_remote_copy(
            src_ref=part,
            dst_ref=parts.at[shift],
            send_sem=part_send.at[shift],
            recv_sem=part_recv.at[shift],
            device_id={"prow": to},
            device_id_type=MESH,
        )

    for shift in range(1, count):
        share(shift).start()

    for s in range(supers):
        if wide == 2:
            send(s, me, ACROSS, sibling, True).wait_send()

        @pl.when(has_up)
        def _():
            send(s, me, UP, up, True).wait_send()

        @pl.when(has_down)
        def _():
            send(s, me, DOWN, down, True).wait_send()

    def left(d, _):
        above, below = z + d, z - d
        for s in range(supers):
            @pl.when(above < line)
            def _():
                @pl.when(has_down)
                def _():
                    send(s, at(above, y), DOWN, down).wait_send()

                if wide == 2:
                    @pl.when(crosses(s, above))
                    def _():
                        send(s, at(above, y), ACROSS, sibling).wait_send()

            @pl.when(below >= 0)
            def _():
                @pl.when(has_up)
                def _():
                    send(s, at(below, y), UP, up).wait_send()

                if wide == 2:
                    @pl.when(crosses(s, below))
                    def _():
                        send(s, at(below, y), ACROSS, sibling).wait_send()
        return 0

    lax.fori_loop(1, line, left, 0)
    if wide == 2:
        extra.wait_send()
    swap.wait_send()

    total = diag[...] - part[...]
    for shift in range(1, count):
        share(shift).wait()
        total = total - parts[shift]
    variance[...] = total


def per_device(line, wide, inverse_tiles, panel_blocks, diag_inverse, structure, block_slot):
    rows, columns, tile, _ = inverse_tiles.shape
    supers, held, _, width = panel_blocks.shape
    count = line * wide
    bf16, f32 = jnp.bfloat16, jnp.float32
    dma = pltpu.SemaphoreType.DMA
    whole = pl.BlockSpec(memory_space=pltpu.VMEM)
    scalars = pl.BlockSpec(memory_space=pltpu.SMEM)
    anywhere = pl.BlockSpec(memory_space=pl.ANY)
    flops = 2 * supers * rows * tile * width * tile * structure.shape[1]
    return pl.pallas_call(
        functools.partial(kernel, line, wide),
        out_shape=(
            jax.ShapeDtypeStruct((supers, rows, tile, width), bf16),
            jax.ShapeDtypeStruct((supers, width), f32),
        ),
        in_specs=[scalars, scalars, anywhere, anywhere, whole],
        out_specs=(whole, whole),
        scratch_shapes=[
            pltpu.VMEM((rows, 2 * columns, tile, tile), bf16),
            pltpu.VMEM((supers, rows * tile, width), f32),
            pltpu.VMEM((supers, width), f32),
            pltpu.VMEM((count, supers, width), f32),
            *[pltpu.VMEM((count, held, tile, width), bf16) for _ in range(supers)],
            dma((supers,)),
            dma((4, supers, count)),
            dma((supers, count)),
            dma,
            dma,
            dma,
            dma((count,)),
            dma((count,)),
        ],
        compiler_params=pltpu.CompilerParams(
            collective_id=0, has_side_effects=True, vmem_limit_bytes=48 * 2**20
        ),
        cost_estimate=pl.CostEstimate(
            flops=flops, bytes_accessed=4 * inverse_tiles.size, transcendentals=0
        ),
    )(structure, block_slot, inverse_tiles, panel_blocks, diag_inverse)


def solution(mesh):
    line, wide = grid_of(mesh)
    in_specs = (
        P(("fields", "prow"), "pcol", None, None),
        P("fields", "prow", None, "pcol"),
        P("fields", "pcol"),
        P("fields", None),
        P("fields"),
    )
    out_specs = (P("fields", "prow", None, "pcol"), P("fields", "pcol"))
    return jax.shard_map(
        functools.partial(per_device, line, wide),
        mesh=mesh, in_specs=in_specs, out_specs=out_specs, check_vma=False,
    )
```

```python
import functools

import jax
import jax.numpy as jnp
from jax import lax
from jax.experimental import pallas as pl
from jax.experimental.pallas import tpu as pltpu
from jax.sharding import PartitionSpec as P

MESH = pl.DeviceIdType.MESH
UP, DOWN, ACROSS, EXTRA = range(4)


def grid_of(mesh):
    count = mesh.shape["prow"]
    line = None
    devices = getattr(mesh, "devices", None)
    if devices is not None and hasattr(devices.flat[0], "coords"):
        line = len({tuple(d.coords)[2] for d in devices[0, :, 0]})
    if line is None and count % 2 == 0:
        line = count // 2
    if line is None or line * 2 != count or line % 2:
        return count, 1
    return line, 2


def kernel(
    line, wide, structure_in, block_slot_in, tiles, panel, diag_in, sigma_out, variance,
    structure, block_slot, diag, list_sem, sigma, sigma_sem, full, acc, part, parts, *rest,
):
    supers = structure.shape[0]
    positions = structure.shape[1]
    rows, columns, tile = tiles.shape[0], tiles.shape[1], tiles.shape[2]
    width = panel.shape[3]
    held = positions // (line * wide)
    count = line * wide
    panels = rest[:supers]
    (
        panel_sem, send_sem, recv_sem, tile_sem, tile_send, tile_recv,
        part_send, part_recv,
    ) = rest[supers:]

    me = lax.axis_index("prow")
    core = lax.axis_index("pcol")
    z, y = me // wide, me % wide
    sibling = z * wide + (wide - 1 - y)
    twin = (z + 1 - 2 * (z % 2)) * wide + y
    last = supers - 1

    def at(zz, yy):
        return zz * wide + yy

    barrier = pltpu.get_barrier_semaphore()
    up, down = at(z + 1, y), at(z - 1, y)
    has_up, has_down = z + 1 < line, z >= 1

    def greet(place):
        pl.semaphore_signal(barrier, inc=1, device_id=place, device_id_type=MESH)

    @pl.when(has_up)
    def _():
        greet({"prow": up})

    @pl.when(has_down)
    def _():
        greet({"prow": down})

    if wide == 2:
        greet({"prow": sibling})
    greet({"pcol": 1 - core})
    lists = [
        pltpu.make_async_copy(structure_in, structure, list_sem.at[0]),
        pltpu.make_async_copy(block_slot_in, block_slot, list_sem.at[1]),
    ]
    lists.append(pltpu.make_async_copy(diag_in, diag, list_sem.at[2]))
    for copy in lists:
        copy.start()
    pl.semaphore_wait(
        barrier, wide + jnp.where(has_up, 1, 0) + jnp.where(has_down, 1, 0)
    )

    def send(s, source, kind, to, own=False):
        return pltpu.make_async_remote_copy(
            src_ref=panel.at[s] if own else panels[s].at[source],
            dst_ref=panels[s].at[source],
            send_sem=send_sem.at[kind, s, source],
            recv_sem=recv_sem.at[s, source],
            device_id={"prow": to},
            device_id_type=MESH,
        )

    def arrive(s, source):
        send(s, source, UP, me).wait_recv()

    for s in range(supers):
        if wide == 2:
            send(s, me, ACROSS, sibling, True).start()

        @pl.when(has_up)
        def _():
            send(s, me, UP, up, True).start()

        @pl.when(has_down)
        def _():
            send(s, me, DOWN, down, True).start()

    swap = pltpu.make_async_remote_copy(
        src_ref=tiles,
        dst_ref=full.at[:, pl.ds(core * columns, columns)],
        send_sem=tile_send,
        recv_sem=tile_recv,
        device_id={"pcol": 1 - core},
        device_id_type=MESH,
    )
    swap.start()
    keep = pltpu.make_async_copy(
        tiles, full.at[:, pl.ds(core * columns, columns)], tile_sem
    )
    keep.start()
    own = [
        pltpu.make_async_copy(panel.at[s], panels[s].at[me], panel_sem.at[s])
        for s in range(supers)
    ]
    for s in range(supers):
        own[s].start()
    for s in range(supers):
        acc[s] = jnp.zeros(acc.shape[1:], acc.dtype)

    def add(s, source):
        for k in range(held):
            slot = block_slot[structure[s, source * held + k]]
            left = full[:, slot].reshape(rows * tile, tile)
            acc[s] += jnp.dot(
                left, panels[s][source, k], preferred_element_type=jnp.float32
            )

    def crosses(s, zz):
        if s != last:
            return zz >= 0
        return zz != z + 1 - 2 * (z % 2)

    def flush():
        for copy in lists:
            copy.wait()
        for s in range(supers):
            own[s].wait()
        keep.wait()
        swap.wait_recv()
        for s in range(supers):
            add(s, me)

    def step(d, _):
        above, below = z + d, z - d
        for s in range(supers):
            @pl.when(above < line)
            def _():
                arrive(s, at(above, y))

                @pl.when(has_down)
                def _():
                    send(s, at(above, y), DOWN, down).start()

                if wide == 2:
                    @pl.when(crosses(s, above))
                    def _():
                        send(s, at(above, y), ACROSS, sibling).start()

            @pl.when(below >= 0)
            def _():
                arrive(s, at(below, y))

                @pl.when(has_up)
                def _():
                    send(s, at(below, y), UP, up).start()

                if wide == 2:
                    @pl.when(crosses(s, below))
                    def _():
                        send(s, at(below, y), ACROSS, sibling).start()

            if s == 0:
                @pl.when(d == 1)
                def _():
                    flush()

            @pl.when(above < line)
            def _():
                add(s, at(above, y))

            @pl.when(below >= 0)
            def _():
                add(s, at(below, y))

            if wide == 2:
                across(s, d - 1)
        return 0

    def across(s, d):
        above, below = z + d, z - d

        @pl.when((above < line) & crosses(s, above))
        def _():
            arrive(s, at(above, 1 - y))
            add(s, at(above, 1 - y))

        @pl.when((below >= 0) & crosses(s, below) & (d > 0))
        def _():
            arrive(s, at(below, 1 - y))
            add(s, at(below, 1 - y))

    lax.fori_loop(1, line, step, 0)

    if wide == 2:
        extra = send(last, sibling, EXTRA, twin)
        extra.start()

    written = [
        pltpu.make_async_copy(sigma.at[s], sigma_out.at[s], sigma_sem.at[s])
        for s in range(supers)
    ]

    def finish(s):
        total = jnp.zeros((1, width), jnp.float32)
        for r in range(rows):
            row = me * rows + r
            position, used = jnp.int32(0), jnp.int32(0)
            for a in range(positions):
                hit = block_slot[structure[s, a]] == row
                position = jnp.where(hit, a, position)
                used = jnp.where(hit, 1, used)
            value = jnp.where(used > 0, -acc[s, r * tile:(r + 1) * tile, :], 0.0)
            sigma[s, r] = value.astype(sigma.dtype)
            mine = panels[s][position // held, position % held].astype(jnp.float32)
            total = total + jnp.sum(mine * value, axis=0, keepdims=True)
        part[s:s + 1, :] = total

    for s in range(supers):
        if wide == 2:
            across(s, line - 1)
            if s == last:
                arrive(s, at(z + 1 - 2 * (z % 2), 1 - y))
                add(s, at(z + 1 - 2 * (z % 2), 1 - y))
        finish(s)
        written[s].start()

    def share(shift):
        to = lax.rem(me + shift, count)
        return pltpu.make_async_remote_copy(
            src_ref=part,
            dst_ref=parts.at[shift],
            send_sem=part_send.at[shift],
            recv_sem=part_recv.at[shift],
            device_id={"prow": to},
            device_id_type=MESH,
        )

    for shift in range(1, count):
        share(shift).start()

    for s in range(supers):
        if wide == 2:
            send(s, me, ACROSS, sibling, True).wait_send()

        @pl.when(has_up)
        def _():
            send(s, me, UP, up, True).wait_send()

        @pl.when(has_down)
        def _():
            send(s, me, DOWN, down, True).wait_send()

    def left(d, _):
        above, below = z + d, z - d
        for s in range(supers):
            @pl.when(above < line)
            def _():
                @pl.when(has_down)
                def _():
                    send(s, at(above, y), DOWN, down).wait_send()

                if wide == 2:
                    @pl.when(crosses(s, above))
                    def _():
                        send(s, at(above, y), ACROSS, sibling).wait_send()

            @pl.when(below >= 0)
            def _():
                @pl.when(has_up)
                def _():
                    send(s, at(below, y), UP, up).wait_send()

                if wide == 2:
                    @pl.when(crosses(s, below))
                    def _():
                        send(s, at(below, y), ACROSS, sibling).wait_send()
        return 0

    lax.fori_loop(1, line, left, 0)
    if wide == 2:
        extra.wait_send()
    swap.wait_send()

    total = diag[...] - part[...]
    for shift in range(1, count):
        share(shift).wait()
        total = total - parts[shift]
    variance[...] = total
    for s in range(supers):
        written[s].wait()


def per_device(line, wide, inverse_tiles, panel_blocks, diag_inverse, structure, block_slot):
    rows, columns, tile, _ = inverse_tiles.shape
    supers, held, _, width = panel_blocks.shape
    count = line * wide
    bf16, f32 = jnp.bfloat16, jnp.float32
    dma = pltpu.SemaphoreType.DMA
    whole = pl.BlockSpec(memory_space=pltpu.VMEM)
    outside = pl.BlockSpec(memory_space=pltpu.HBM)
    flops = 2 * supers * rows * tile * width * tile * structure.shape[1]
    return pl.pallas_call(
        functools.partial(kernel, line, wide),
        out_shape=(
            jax.ShapeDtypeStruct((supers, rows, tile, width), bf16),
            jax.ShapeDtypeStruct((supers, width), f32),
        ),
        in_specs=[outside] * 5,
        out_specs=(outside, whole),
        scratch_shapes=[
            pltpu.SMEM(structure.shape, structure.dtype),
            pltpu.SMEM(block_slot.shape, block_slot.dtype),
            pltpu.VMEM(diag_inverse.shape, f32),
            dma((3,)),
            pltpu.VMEM((supers, rows, tile, width), bf16),
            dma((supers,)),
            pltpu.VMEM((rows, 2 * columns, tile, tile), bf16),
            pltpu.VMEM((supers, rows * tile, width), f32),
            pltpu.VMEM((supers, width), f32),
            pltpu.VMEM((count, supers, width), f32),
            *[pltpu.VMEM((count, held, tile, width), bf16) for _ in range(supers)],
            dma((supers,)),
            dma((4, supers, count)),
            dma((supers, count)),
            dma,
            dma,
            dma,
            dma((count,)),
            dma((count,)),
        ],
        compiler_params=pltpu.CompilerParams(
            collective_id=0, has_side_effects=True, vmem_limit_bytes=60 * 2**20
        ),
        cost_estimate=pl.CostEstimate(
            flops=flops, bytes_accessed=4 * inverse_tiles.size, transcendentals=0
        ),
    )(structure, block_slot, inverse_tiles, panel_blocks, diag_inverse)


def solution(mesh):
    line, wide = grid_of(mesh)
    in_specs = (
        P(("fields", "prow"), "pcol", None, None),
        P("fields", "prow", None, "pcol"),
        P("fields", "pcol"),
        P("fields", None),
        P("fields"),
    )
    out_specs = (P("fields", "prow", None, "pcol"), P("fields", "pcol"))
    return jax.shard_map(
        functools.partial(per_device, line, wide),
        mesh=mesh, in_specs=in_specs, out_specs=out_specs, check_vma=False,
    )
```

```python
import functools

import jax
import jax.numpy as jnp
from jax import lax
from jax.experimental import pallas as pl
from jax.experimental.pallas import tpu as pltpu
from jax.sharding import PartitionSpec as P

MESH = pl.DeviceIdType.MESH
UP, DOWN, ACROSS, EXTRA = range(4)
PIECES = 2


def grid_of(mesh):
    count = mesh.shape["prow"]
    line = None
    devices = getattr(mesh, "devices", None)
    if devices is not None and hasattr(devices.flat[0], "coords"):
        line = len({tuple(d.coords)[2] for d in devices[0, :, 0]})
    if line is None and count % 2 == 0:
        line = count // 2
    if line is None or line * 2 != count or line % 2:
        return count, 1
    return line, 2


def kernel(
    line, wide, structure_in, block_slot_in, tiles, panel, diag_in, sigma, variance,
    structure, block_slot, diag, list_sem, full, acc, part, parts, *rest,
):
    supers = structure.shape[0]
    positions = structure.shape[1]
    rows, columns, tile = tiles.shape[0], tiles.shape[1], tiles.shape[2]
    width = panel.shape[3]
    held = positions // (line * wide)
    count = line * wide
    panels = rest[:supers]
    (
        panel_sem, send_sem, recv_sem, tile_sem, tile_send, tile_recv,
        part_send, part_recv,
    ) = rest[supers:]

    me = lax.axis_index("prow")
    core = lax.axis_index("pcol")
    z, y = me // wide, me % wide
    sibling = z * wide + (wide - 1 - y)
    twin = (z + 1 - 2 * (z % 2)) * wide + y
    last = supers - 1
    depth = tile // PIECES
    chunks = [(s, h) for s in range(supers) for h in range(PIECES)]

    def at(zz, yy):
        return zz * wide + yy

    barrier = pltpu.get_barrier_semaphore()
    up, down = at(z + 1, y), at(z - 1, y)
    has_up, has_down = z + 1 < line, z >= 1

    def greet(place):
        pl.semaphore_signal(barrier, inc=1, device_id=place, device_id_type=MESH)

    @pl.when(has_up)
    def _():
        greet({"prow": up})

    @pl.when(has_down)
    def _():
        greet({"prow": down})

    if wide == 2:
        greet({"prow": sibling})
    greet({"pcol": 1 - core})
    lists = [
        pltpu.make_async_copy(structure_in, structure, list_sem.at[0]),
        pltpu.make_async_copy(block_slot_in, block_slot, list_sem.at[1]),
    ]
    lists.append(pltpu.make_async_copy(diag_in, diag, list_sem.at[2]))
    for copy in lists:
        copy.start()
    pl.semaphore_wait(
        barrier, wide + jnp.where(has_up, 1, 0) + jnp.where(has_down, 1, 0)
    )

    def send(c, source, kind, to, own=False):
        s, h = c
        piece = pl.ds(h * depth, depth)
        target = panels[s].at[source, :, piece]
        return pltpu.make_async_remote_copy(
            src_ref=panel.at[s, :, piece] if own else target,
            dst_ref=target,
            send_sem=send_sem.at[kind, s * PIECES + h, source],
            recv_sem=recv_sem.at[s * PIECES + h, source],
            device_id={"prow": to},
            device_id_type=MESH,
        )

    def arrive(c, source):
        send(c, source, UP, me).wait_recv()

    for c in chunks:
        if wide == 2:
            send(c, me, ACROSS, sibling, True).start()

        @pl.when(has_up)
        def _():
            send(c, me, UP, up, True).start()

        @pl.when(has_down)
        def _():
            send(c, me, DOWN, down, True).start()

    swap = pltpu.make_async_remote_copy(
        src_ref=tiles,
        dst_ref=full.at[:, pl.ds(core * columns, columns)],
        send_sem=tile_send,
        recv_sem=tile_recv,
        device_id={"pcol": 1 - core},
        device_id_type=MESH,
    )
    swap.start()
    keep = pltpu.make_async_copy(
        tiles, full.at[:, pl.ds(core * columns, columns)], tile_sem
    )
    keep.start()
    own = [
        pltpu.make_async_copy(panel.at[s], panels[s].at[me], panel_sem.at[s])
        for s in range(supers)
    ]
    for s in range(supers):
        own[s].start()
    for s in range(supers):
        acc[s] = jnp.zeros(acc.shape[1:], acc.dtype)

    def add(s, source):
        for k in range(held):
            slot = block_slot[structure[s, source * held + k]]
            left = full[:, slot].reshape(rows * tile, tile)
            acc[s] += jnp.dot(
                left, panels[s][source, k], preferred_element_type=jnp.float32
            )

    def crosses(s, zz):
        if s != last:
            return zz >= 0
        return zz != z + 1 - 2 * (z % 2)

    def flush():
        for copy in lists:
            copy.wait()
        for s in range(supers):
            own[s].wait()
        keep.wait()
        swap.wait_recv()
        for s in range(supers):
            add(s, me)
            add_both(s, 1)

    def pass_on(c, d):
        above, below = z + d, z - d

        @pl.when(above < line)
        def _():
            arrive(c, at(above, y))

            @pl.when(has_down)
            def _():
                send(c, at(above, y), DOWN, down).start()

            if wide == 2:
                @pl.when(crosses(c[0], above))
                def _():
                    send(c, at(above, y), ACROSS, sibling).start()

        @pl.when(below >= 0)
        def _():
            arrive(c, at(below, y))

            @pl.when(has_up)
            def _():
                send(c, at(below, y), UP, up).start()

            if wide == 2:
                @pl.when(crosses(c[0], below))
                def _():
                    send(c, at(below, y), ACROSS, sibling).start()

    def add_both(s, d):
        above, below = z + d, z - d

        @pl.when(above < line)
        def _():
            add(s, at(above, y))

        @pl.when(below >= 0)
        def _():
            add(s, at(below, y))

    def step(d, _):
        for s in range(supers):
            for h in range(PIECES):
                pass_on((s, h), d)
            if s == last:
                @pl.when(d == 1)
                def _():
                    flush()

            @pl.when(d > 1)
            def _():
                add_both(s, d)
        return 0

    lax.fori_loop(1, line, step, 0)

    def arrive_all(s, source):
        for h in range(PIECES):
            arrive((s, h), source)

    def across(s, d):
        above, below = z + d, z - d

        @pl.when((above < line) & crosses(s, above))
        def _():
            arrive_all(s, at(above, 1 - y))
            add(s, at(above, 1 - y))

        @pl.when((below >= 0) & crosses(s, below))
        def _():
            arrive_all(s, at(below, 1 - y))
            add(s, at(below, 1 - y))

    if wide == 2:
        extra = [send((last, h), sibling, EXTRA, twin) for h in range(PIECES)]
        for h in range(PIECES):
            arrive((last, h), sibling)
            extra[h].start()
        for s in range(supers):
            if s != last:
                arrive_all(s, sibling)
            add(s, sibling)

        def later(d, _):
            for s in range(supers):
                across(s, d)
            return 0

        lax.fori_loop(1, line - 1, later, 0)

    def finish(s):
        total = jnp.zeros((1, width), jnp.float32)
        for r in range(rows):
            row = me * rows + r
            position, used = jnp.int32(0), jnp.int32(0)
            for a in range(positions):
                hit = block_slot[structure[s, a]] == row
                position = jnp.where(hit, a, position)
                used = jnp.where(hit, 1, used)
            value = jnp.where(used > 0, -acc[s, r * tile:(r + 1) * tile, :], 0.0)
            sigma[s, r] = value.astype(sigma.dtype)
            mine = panels[s][position // held, position % held].astype(jnp.float32)
            total = total + jnp.sum(mine * value, axis=0, keepdims=True)
        part[s:s + 1, :] = total

    for s in range(supers):
        if wide == 2:
            across(s, line - 1)
            if s == last:
                arrive_all(s, at(z + 1 - 2 * (z % 2), 1 - y))
                add(s, at(z + 1 - 2 * (z % 2), 1 - y))
        finish(s)

    def share(shift):
        to = lax.rem(me + shift, count)
        return pltpu.make_async_remote_copy(
            src_ref=part,
            dst_ref=parts.at[shift],
            send_sem=part_send.at[shift],
            recv_sem=part_recv.at[shift],
            device_id={"prow": to},
            device_id_type=MESH,
        )

    for shift in range(1, count):
        share(shift).start()

    for c in chunks:
        if wide == 2:
            send(c, me, ACROSS, sibling, True).wait_send()

        @pl.when(has_up)
        def _():
            send(c, me, UP, up, True).wait_send()

        @pl.when(has_down)
        def _():
            send(c, me, DOWN, down, True).wait_send()

    def left(d, _):
        above, below = z + d, z - d
        for c in chunks:
            @pl.when(above < line)
            def _():
                @pl.when(has_down)
                def _():
                    send(c, at(above, y), DOWN, down).wait_send()

                if wide == 2:
                    @pl.when(crosses(c[0], above))
                    def _():
                        send(c, at(above, y), ACROSS, sibling).wait_send()

            @pl.when(below >= 0)
            def _():
                @pl.when(has_up)
                def _():
                    send(c, at(below, y), UP, up).wait_send()

                if wide == 2:
                    @pl.when(crosses(c[0], below))
                    def _():
                        send(c, at(below, y), ACROSS, sibling).wait_send()
        return 0

    lax.fori_loop(1, line, left, 0)
    if wide == 2:
        for h in range(PIECES):
            extra[h].wait_send()
    swap.wait_send()

    total = diag[...] - part[...]
    for shift in range(1, count):
        share(shift).wait()
        total = total - parts[shift]
    variance[...] = total


def per_device(line, wide, inverse_tiles, panel_blocks, diag_inverse, structure, block_slot):
    rows, columns, tile, _ = inverse_tiles.shape
    supers, held, _, width = panel_blocks.shape
    count = line * wide
    bf16, f32 = jnp.bfloat16, jnp.float32
    dma = pltpu.SemaphoreType.DMA
    whole = pl.BlockSpec(memory_space=pltpu.VMEM)
    outside = pl.BlockSpec(memory_space=pltpu.HBM)
    flops = 2 * supers * rows * tile * width * tile * structure.shape[1]
    return pl.pallas_call(
        functools.partial(kernel, line, wide),
        out_shape=(
            pltpu.VMEM((supers, rows, tile, width), bf16),
            pltpu.VMEM((supers, width), f32),
        ),
        in_specs=[outside] * 5,
        out_specs=(whole, whole),
        scratch_shapes=[
            pltpu.SMEM(structure.shape, structure.dtype),
            pltpu.SMEM(block_slot.shape, block_slot.dtype),
            pltpu.VMEM(diag_inverse.shape, f32),
            dma((3,)),
            pltpu.VMEM((rows, 2 * columns, tile, tile), bf16),
            pltpu.VMEM((supers, rows * tile, width), f32),
            pltpu.VMEM((supers, width), f32),
            pltpu.VMEM((count, supers, width), f32),
            *[pltpu.VMEM((count, held, tile, width), bf16) for _ in range(supers)],
            dma((supers,)),
            dma((4, supers * PIECES, count)),
            dma((supers * PIECES, count)),
            dma,
            dma,
            dma,
            dma((count,)),
            dma((count,)),
        ],
        compiler_params=pltpu.CompilerParams(
            collective_id=0, has_side_effects=True, vmem_limit_bytes=60 * 2**20
        ),
        cost_estimate=pl.CostEstimate(
            flops=flops, bytes_accessed=4 * inverse_tiles.size, transcendentals=0
        ),
    )(structure, block_slot, inverse_tiles, panel_blocks, diag_inverse)


def solution(mesh):
    line, wide = grid_of(mesh)
    in_specs = (
        P(("fields", "prow"), "pcol", None, None),
        P("fields", "prow", None, "pcol"),
        P("fields", "pcol"),
        P("fields", None),
        P("fields"),
    )
    out_specs = (P("fields", "prow", None, "pcol"), P("fields", "pcol"))
    return jax.shard_map(
        functools.partial(per_device, line, wide),
        mesh=mesh, in_specs=in_specs, out_specs=out_specs, check_vma=False,
    )
```

```python
import functools

import jax
import jax.numpy as jnp
from jax import lax
from jax.experimental import pallas as pl
from jax.experimental.pallas import tpu as pltpu
from jax.sharding import PartitionSpec as P

MESH = pl.DeviceIdType.MESH
UP, DOWN, ACROSS, EXTRA = range(4)
PIECES = 4


def grid_of(mesh):
    count = mesh.shape["prow"]
    line = None
    devices = getattr(mesh, "devices", None)
    if devices is not None and hasattr(devices.flat[0], "coords"):
        line = len({tuple(d.coords)[2] for d in devices[0, :, 0]})
    if line is None and count % 2 == 0:
        line = count // 2
    if line is None or line * 2 != count or line % 2:
        return count, 1
    return line, 2


def kernel(
    line, wide, structure_in, block_slot_in, tiles, panel, diag_in, sigma, variance,
    structure, block_slot, diag, list_sem, full, acc, part, parts, *rest,
):
    supers = structure.shape[0]
    positions = structure.shape[1]
    rows, columns, tile = tiles.shape[0], tiles.shape[1], tiles.shape[2]
    width = panel.shape[3]
    held = positions // (line * wide)
    count = line * wide
    panels = rest[:supers]
    (
        panel_sem, send_sem, recv_sem, tile_sem, tile_send, tile_recv,
        part_send, part_recv,
    ) = rest[supers:]

    me = lax.axis_index("prow")
    core = lax.axis_index("pcol")
    z, y = me // wide, me % wide
    sibling = z * wide + (wide - 1 - y)
    twin = (z + 1 - 2 * (z % 2)) * wide + y
    last = supers - 1
    first = min(2, line - 1)
    depth = tile // PIECES
    chunks = [(s, h) for s in range(supers) for h in range(PIECES)]

    def at(zz, yy):
        return zz * wide + yy

    barrier = pltpu.get_barrier_semaphore()
    up, down = at(z + 1, y), at(z - 1, y)
    has_up, has_down = z + 1 < line, z >= 1

    def greet(place):
        pl.semaphore_signal(barrier, inc=1, device_id=place, device_id_type=MESH)

    @pl.when(has_up)
    def _():
        greet({"prow": up})

    @pl.when(has_down)
    def _():
        greet({"prow": down})

    if wide == 2:
        greet({"prow": sibling})
    greet({"pcol": 1 - core})
    lists = [
        pltpu.make_async_copy(structure_in, structure, list_sem.at[0]),
        pltpu.make_async_copy(block_slot_in, block_slot, list_sem.at[1]),
    ]
    lists.append(pltpu.make_async_copy(diag_in, diag, list_sem.at[2]))
    for copy in lists:
        copy.start()
    pl.semaphore_wait(
        barrier, wide + jnp.where(has_up, 1, 0) + jnp.where(has_down, 1, 0)
    )

    def send(c, source, kind, to, own=False):
        s, h = c
        piece = pl.ds(h * depth, depth)
        target = panels[s].at[source, :, piece]
        return pltpu.make_async_remote_copy(
            src_ref=panel.at[s, :, piece] if own else target,
            dst_ref=target,
            send_sem=send_sem.at[kind, s * PIECES + h, source],
            recv_sem=recv_sem.at[s * PIECES + h, source],
            device_id={"prow": to},
            device_id_type=MESH,
        )

    def arrive(c, source):
        send(c, source, UP, me).wait_recv()

    for c in chunks:
        if wide == 2:
            send(c, me, ACROSS, sibling, True).start()

        @pl.when(has_up)
        def _():
            send(c, me, UP, up, True).start()

        @pl.when(has_down)
        def _():
            send(c, me, DOWN, down, True).start()

    swap = pltpu.make_async_remote_copy(
        src_ref=tiles,
        dst_ref=full.at[:, pl.ds(core * columns, columns)],
        send_sem=tile_send,
        recv_sem=tile_recv,
        device_id={"pcol": 1 - core},
        device_id_type=MESH,
    )
    swap.start()
    keep = pltpu.make_async_copy(
        tiles, full.at[:, pl.ds(core * columns, columns)], tile_sem
    )
    keep.start()
    own = [
        pltpu.make_async_copy(panel.at[s], panels[s].at[me], panel_sem.at[s])
        for s in range(supers)
    ]
    for s in range(supers):
        own[s].start()
    for s in range(supers):
        acc[s] = jnp.zeros(acc.shape[1:], acc.dtype)

    def add(s, source):
        for k in range(held):
            slot = block_slot[structure[s, source * held + k]]
            left = full[:, slot].reshape(rows * tile, tile)
            acc[s] += jnp.dot(
                left, panels[s][source, k], preferred_element_type=jnp.float32
            )

    def crosses(s, zz):
        if s != last:
            return zz >= 0
        return zz != z + 1 - 2 * (z % 2)

    def flush():
        for copy in lists:
            copy.wait()
        for s in range(supers):
            own[s].wait()
        keep.wait()
        swap.wait_recv()
        for s in range(supers):
            add(s, me)
            for d in range(1, first + 1):
                add_both(s, d)

    def pass_on(c, d):
        above, below = z + d, z - d

        @pl.when(above < line)
        def _():
            arrive(c, at(above, y))

            @pl.when(has_down)
            def _():
                send(c, at(above, y), DOWN, down).start()

            if wide == 2:
                @pl.when(crosses(c[0], above))
                def _():
                    send(c, at(above, y), ACROSS, sibling).start()

        @pl.when(below >= 0)
        def _():
            arrive(c, at(below, y))

            @pl.when(has_up)
            def _():
                send(c, at(below, y), UP, up).start()

            if wide == 2:
                @pl.when(crosses(c[0], below))
                def _():
                    send(c, at(below, y), ACROSS, sibling).start()

    def add_both(s, d):
        above, below = z + d, z - d

        @pl.when(above < line)
        def _():
            add(s, at(above, y))

        @pl.when(below >= 0)
        def _():
            add(s, at(below, y))

    def step(d, _):
        for s in range(supers):
            for h in range(PIECES):
                pass_on((s, h), d)
            if s == last:
                @pl.when(d == first)
                def _():
                    flush()

            @pl.when(d > first)
            def _():
                add_both(s, d)
        return 0

    lax.fori_loop(1, line, step, 0)

    def arrive_all(s, source):
        for h in range(PIECES):
            arrive((s, h), source)

    def across(s, d):
        above, below = z + d, z - d

        @pl.when((above < line) & crosses(s, above))
        def _():
            arrive_all(s, at(above, 1 - y))
            add(s, at(above, 1 - y))

        @pl.when((below >= 0) & crosses(s, below))
        def _():
            arrive_all(s, at(below, 1 - y))
            add(s, at(below, 1 - y))

    if wide == 2:
        extra = [send((last, h), sibling, EXTRA, twin) for h in range(PIECES)]
        for h in range(PIECES):
            arrive((last, h), sibling)
            extra[h].start()
        for s in range(supers):
            if s != last:
                arrive_all(s, sibling)
            add(s, sibling)

        def later(d, _):
            for s in range(supers):
                across(s, d)
            return 0

        lax.fori_loop(1, line - 1, later, 0)

    def finish(s):
        total = jnp.zeros((1, width), jnp.float32)
        for r in range(rows):
            row = me * rows + r
            position, used = jnp.int32(0), jnp.int32(0)
            for a in range(positions):
                hit = block_slot[structure[s, a]] == row
                position = jnp.where(hit, a, position)
                used = jnp.where(hit, 1, used)
            value = jnp.where(used > 0, -acc[s, r * tile:(r + 1) * tile, :], 0.0)
            sigma[s, r] = value.astype(sigma.dtype)
            mine = panels[s][position // held, position % held].astype(jnp.float32)
            total = total + jnp.sum(mine * value, axis=0, keepdims=True)
        part[s:s + 1, :] = total

    for s in range(supers):
        if wide == 2:
            across(s, line - 1)
            if s == last:
                arrive_all(s, at(z + 1 - 2 * (z % 2), 1 - y))
                add(s, at(z + 1 - 2 * (z % 2), 1 - y))
        finish(s)

    def share(shift):
        to = lax.rem(me + shift, count)
        return pltpu.make_async_remote_copy(
            src_ref=part,
            dst_ref=parts.at[shift],
            send_sem=part_send.at[shift],
            recv_sem=part_recv.at[shift],
            device_id={"prow": to},
            device_id_type=MESH,
        )

    for shift in range(1, count):
        share(shift).start()

    for c in chunks:
        if wide == 2:
            send(c, me, ACROSS, sibling, True).wait_send()

        @pl.when(has_up)
        def _():
            send(c, me, UP, up, True).wait_send()

        @pl.when(has_down)
        def _():
            send(c, me, DOWN, down, True).wait_send()

    def left(d, _):
        above, below = z + d, z - d
        for c in chunks:
            @pl.when(above < line)
            def _():
                @pl.when(has_down)
                def _():
                    send(c, at(above, y), DOWN, down).wait_send()

                if wide == 2:
                    @pl.when(crosses(c[0], above))
                    def _():
                        send(c, at(above, y), ACROSS, sibling).wait_send()

            @pl.when(below >= 0)
            def _():
                @pl.when(has_up)
                def _():
                    send(c, at(below, y), UP, up).wait_send()

                if wide == 2:
                    @pl.when(crosses(c[0], below))
                    def _():
                        send(c, at(below, y), ACROSS, sibling).wait_send()
        return 0

    lax.fori_loop(1, line, left, 0)
    if wide == 2:
        for h in range(PIECES):
            extra[h].wait_send()
    swap.wait_send()

    total = diag[...] - part[...]
    for shift in range(1, count):
        share(shift).wait()
        total = total - parts[shift]
    variance[...] = total


def per_device(line, wide, inverse_tiles, panel_blocks, diag_inverse, structure, block_slot):
    rows, columns, tile, _ = inverse_tiles.shape
    supers, held, _, width = panel_blocks.shape
    count = line * wide
    bf16, f32 = jnp.bfloat16, jnp.float32
    dma = pltpu.SemaphoreType.DMA
    whole = pl.BlockSpec(memory_space=pltpu.VMEM)
    outside = pl.BlockSpec(memory_space=pltpu.HBM)
    flops = 2 * supers * rows * tile * width * tile * structure.shape[1]
    return pl.pallas_call(
        functools.partial(kernel, line, wide),
        out_shape=(
            pltpu.VMEM((supers, rows, tile, width), bf16),
            pltpu.VMEM((supers, width), f32),
        ),
        in_specs=[outside] * 5,
        out_specs=(whole, whole),
        scratch_shapes=[
            pltpu.SMEM(structure.shape, structure.dtype),
            pltpu.SMEM(block_slot.shape, block_slot.dtype),
            pltpu.VMEM(diag_inverse.shape, f32),
            dma((3,)),
            pltpu.VMEM((rows, 2 * columns, tile, tile), bf16),
            pltpu.VMEM((supers, rows * tile, width), f32),
            pltpu.VMEM((supers, width), f32),
            pltpu.VMEM((count, supers, width), f32),
            *[pltpu.VMEM((count, held, tile, width), bf16) for _ in range(supers)],
            dma((supers,)),
            dma((4, supers * PIECES, count)),
            dma((supers * PIECES, count)),
            dma,
            dma,
            dma,
            dma((count,)),
            dma((count,)),
        ],
        compiler_params=pltpu.CompilerParams(
            collective_id=0, has_side_effects=True, vmem_limit_bytes=60 * 2**20
        ),
        cost_estimate=pl.CostEstimate(
            flops=flops, bytes_accessed=4 * inverse_tiles.size, transcendentals=0
        ),
    )(structure, block_slot, inverse_tiles, panel_blocks, diag_inverse)


def solution(mesh):
    line, wide = grid_of(mesh)
    in_specs = (
        P(("fields", "prow"), "pcol", None, None),
        P("fields", "prow", None, "pcol"),
        P("fields", "pcol"),
        P("fields", None),
        P("fields"),
    )
    out_specs = (P("fields", "prow", None, "pcol"), P("fields", "pcol"))
    return jax.shard_map(
        functools.partial(per_device, line, wide),
        mesh=mesh, in_specs=in_specs, out_specs=out_specs, check_vma=False,
    )
```

```python
import functools

import jax
import jax.numpy as jnp
from jax import lax
from jax.experimental import pallas as pl
from jax.experimental.pallas import tpu as pltpu
from jax.sharding import PartitionSpec as P

MESH = pl.DeviceIdType.MESH
UP, DOWN, ACROSS, EXTRA = range(4)
PIECES = 2


def grid_of(mesh):
    count = mesh.shape["prow"]
    line = None
    devices = getattr(mesh, "devices", None)
    if devices is not None and hasattr(devices.flat[0], "coords"):
        line = len({tuple(d.coords)[2] for d in devices[0, :, 0]})
    if line is None and count % 2 == 0:
        line = count // 2
    if line is None or line * 2 != count or line % 2:
        return count, 1
    return line, 2


def kernel(
    line, wide, structure_in, block_slot_in, tiles, panel, diag_in, sigma, variance,
    structure, block_slot, diag, list_sem, full, acc, part, parts, *rest,
):
    supers = structure.shape[0]
    positions = structure.shape[1]
    rows, columns, tile = tiles.shape[0], tiles.shape[1], tiles.shape[2]
    width = panel.shape[3]
    held = positions // (line * wide)
    count = line * wide
    panels = rest[:supers]
    (
        panel_sem, send_sem, recv_sem, tile_sem, tile_send, tile_recv,
        part_send, part_recv,
    ) = rest[supers:]

    me = lax.axis_index("prow")
    core = lax.axis_index("pcol")
    z, y = me // wide, me % wide
    sibling = z * wide + (wide - 1 - y)
    twin = (z + 1 - 2 * (z % 2)) * wide + y
    last = supers - 1
    depth = tile // PIECES
    chunks = [(s, h) for s in range(supers) for h in range(PIECES)]

    def at(zz, yy):
        return zz * wide + yy

    barrier = pltpu.get_barrier_semaphore()
    up, down = at(z + 1, y), at(z - 1, y)
    has_up, has_down = z + 1 < line, z >= 1

    def greet(place):
        pl.semaphore_signal(barrier, inc=1, device_id=place, device_id_type=MESH)

    @pl.when(has_up)
    def _():
        greet({"prow": up})

    @pl.when(has_down)
    def _():
        greet({"prow": down})

    if wide == 2:
        greet({"prow": sibling})
    greet({"pcol": 1 - core})
    lists = [
        pltpu.make_async_copy(structure_in, structure, list_sem.at[0]),
        pltpu.make_async_copy(block_slot_in, block_slot, list_sem.at[1]),
    ]
    lists.append(pltpu.make_async_copy(diag_in, diag, list_sem.at[2]))
    for copy in lists:
        copy.start()
    pl.semaphore_wait(
        barrier, wide + jnp.where(has_up, 1, 0) + jnp.where(has_down, 1, 0)
    )

    def send(c, source, kind, to, own=False):
        s, h = c
        piece = pl.ds(h * depth, depth)
        target = panels[s].at[source, :, piece]
        return pltpu.make_async_remote_copy(
            src_ref=panel.at[s, :, piece] if own else target,
            dst_ref=target,
            send_sem=send_sem.at[kind, s * PIECES + h, source],
            recv_sem=recv_sem.at[s * PIECES + h, source],
            device_id={"prow": to},
            device_id_type=MESH,
        )

    def arrive(c, source):
        send(c, source, UP, me).wait_recv()

    for c in chunks:
        if wide == 2:
            send(c, me, ACROSS, sibling, True).start()

        @pl.when(has_up)
        def _():
            send(c, me, UP, up, True).start()

        @pl.when(has_down)
        def _():
            send(c, me, DOWN, down, True).start()

    swap = pltpu.make_async_remote_copy(
        src_ref=tiles,
        dst_ref=full.at[:, pl.ds(core * columns, columns)],
        send_sem=tile_send,
        recv_sem=tile_recv,
        device_id={"pcol": 1 - core},
        device_id_type=MESH,
    )
    swap.start()
    keep = pltpu.make_async_copy(
        tiles, full.at[:, pl.ds(core * columns, columns)], tile_sem
    )
    keep.start()
    own = [
        pltpu.make_async_copy(panel.at[s], panels[s].at[me], panel_sem.at[s])
        for s in range(supers)
    ]
    for s in range(supers):
        own[s].start()
    for s in range(supers):
        acc[s] = jnp.zeros(acc.shape[1:], acc.dtype)

    def add(s, source):
        for k in range(held):
            slot = block_slot[structure[s, source * held + k]]
            left = full[:, slot].reshape(rows * tile, tile)
            acc[s] += jnp.dot(
                left, panels[s][source, k], preferred_element_type=jnp.float32
            )

    def crosses(s, zz):
        if s != last:
            return zz >= 0
        return zz != z + 1 - 2 * (z % 2)

    def flush():
        for copy in lists:
            copy.wait()
        for s in range(supers):
            own[s].wait()
        keep.wait()
        swap.wait_recv()
        for s in range(supers):
            add(s, me)
            add_both(s, 1)

    def pass_on(c, d):
        above, below = z + d, z - d

        @pl.when(above < line)
        def _():
            arrive(c, at(above, y))

            @pl.when(has_down)
            def _():
                send(c, at(above, y), DOWN, down).start()

            if wide == 2:
                @pl.when(crosses(c[0], above))
                def _():
                    send(c, at(above, y), ACROSS, sibling).start()

        @pl.when(below >= 0)
        def _():
            arrive(c, at(below, y))

            @pl.when(has_up)
            def _():
                send(c, at(below, y), UP, up).start()

            if wide == 2:
                @pl.when(crosses(c[0], below))
                def _():
                    send(c, at(below, y), ACROSS, sibling).start()

    def add_both(s, d):
        above, below = z + d, z - d

        @pl.when(above < line)
        def _():
            add(s, at(above, y))

        @pl.when(below >= 0)
        def _():
            add(s, at(below, y))

    def step(d, _):
        for s in range(supers):
            for h in range(PIECES):
                pass_on((s, h), d)
            if s == last:
                @pl.when(d == 1)
                def _():
                    flush()

            @pl.when(d > 1)
            def _():
                add_both(s, d)
        return 0

    lax.fori_loop(1, line, step, 0)

    def arrive_all(s, source):
        for h in range(PIECES):
            arrive((s, h), source)

    def across(s, d):
        above, below = z + d, z - d

        @pl.when((above < line) & crosses(s, above))
        def _():
            arrive_all(s, at(above, 1 - y))
            add(s, at(above, 1 - y))

        @pl.when((below >= 0) & crosses(s, below))
        def _():
            arrive_all(s, at(below, 1 - y))
            add(s, at(below, 1 - y))

    for c in chunks:
        @pl.when(has_up)
        def _():
            send(c, me, UP, up, True).wait_send()

        @pl.when(has_down)
        def _():
            send(c, me, DOWN, down, True).wait_send()

    def left_line(d, _):
        above, below = z + d, z - d
        for c in chunks:
            @pl.when((above < line) & has_down)
            def _():
                send(c, at(above, y), DOWN, down).wait_send()

            @pl.when((below >= 0) & has_up)
            def _():
                send(c, at(below, y), UP, up).wait_send()
        return 0

    lax.fori_loop(1, line, left_line, 0)

    if wide == 2:
        extra = [send((last, h), sibling, EXTRA, twin) for h in range(PIECES)]
        for h in range(PIECES):
            arrive((last, h), sibling)
            extra[h].start()
        for s in range(supers):
            if s != last:
                arrive_all(s, sibling)
            add(s, sibling)

        def later(d, _):
            for s in range(supers):
                across(s, d)
            return 0

        lax.fori_loop(1, line - 1, later, 0)

    def finish(s):
        total = jnp.zeros((1, width), jnp.float32)
        for r in range(rows):
            row = me * rows + r
            position, used = jnp.int32(0), jnp.int32(0)
            for a in range(positions):
                hit = block_slot[structure[s, a]] == row
                position = jnp.where(hit, a, position)
                used = jnp.where(hit, 1, used)
            value = jnp.where(used > 0, -acc[s, r * tile:(r + 1) * tile, :], 0.0)
            sigma[s, r] = value.astype(sigma.dtype)
            mine = panels[s][position // held, position % held].astype(jnp.float32)
            total = total + jnp.sum(mine * value, axis=0, keepdims=True)
        part[s:s + 1, :] = total

    for s in range(supers):
        if wide == 2:
            across(s, line - 1)
            if s == last:
                arrive_all(s, at(z + 1 - 2 * (z % 2), 1 - y))
                add(s, at(z + 1 - 2 * (z % 2), 1 - y))
        finish(s)

    def share(shift):
        to = lax.rem(me + shift, count)
        return pltpu.make_async_remote_copy(
            src_ref=part,
            dst_ref=parts.at[shift],
            send_sem=part_send.at[shift],
            recv_sem=part_recv.at[shift],
            device_id={"prow": to},
            device_id_type=MESH,
        )

    for shift in range(1, count):
        share(shift).start()

    if wide == 2:
        for c in chunks:
            send(c, me, ACROSS, sibling, True).wait_send()

        def left_across(d, _):
            above, below = z + d, z - d
            for c in chunks:
                @pl.when((above < line) & crosses(c[0], above))
                def _():
                    send(c, at(above, y), ACROSS, sibling).wait_send()

                @pl.when((below >= 0) & crosses(c[0], below))
                def _():
                    send(c, at(below, y), ACROSS, sibling).wait_send()
            return 0

        lax.fori_loop(1, line, left_across, 0)
    if wide == 2:
        for h in range(PIECES):
            extra[h].wait_send()
    swap.wait_send()

    total = diag[...] - part[...]
    for shift in range(1, count):
        share(shift).wait()
        total = total - parts[shift]
    variance[...] = total


def per_device(line, wide, inverse_tiles, panel_blocks, diag_inverse, structure, block_slot):
    rows, columns, tile, _ = inverse_tiles.shape
    supers, held, _, width = panel_blocks.shape
    count = line * wide
    bf16, f32 = jnp.bfloat16, jnp.float32
    dma = pltpu.SemaphoreType.DMA
    whole = pl.BlockSpec(memory_space=pltpu.VMEM)
    outside = pl.BlockSpec(memory_space=pltpu.HBM)
    flops = 2 * supers * rows * tile * width * tile * structure.shape[1]
    return pl.pallas_call(
        functools.partial(kernel, line, wide),
        out_shape=(
            pltpu.VMEM((supers, rows, tile, width), bf16),
            pltpu.VMEM((supers, width), f32),
        ),
        in_specs=[outside] * 5,
        out_specs=(whole, whole),
        scratch_shapes=[
            pltpu.SMEM(structure.shape, structure.dtype),
            pltpu.SMEM(block_slot.shape, block_slot.dtype),
            pltpu.VMEM(diag_inverse.shape, f32),
            dma((3,)),
            pltpu.VMEM((rows, 2 * columns, tile, tile), bf16),
            pltpu.VMEM((supers, rows * tile, width), f32),
            pltpu.VMEM((supers, width), f32),
            pltpu.VMEM((count, supers, width), f32),
            *[pltpu.VMEM((count, held, tile, width), bf16) for _ in range(supers)],
            dma((supers,)),
            dma((4, supers * PIECES, count)),
            dma((supers * PIECES, count)),
            dma,
            dma,
            dma,
            dma((count,)),
            dma((count,)),
        ],
        compiler_params=pltpu.CompilerParams(
            collective_id=0, has_side_effects=True, vmem_limit_bytes=60 * 2**20
        ),
        cost_estimate=pl.CostEstimate(
            flops=flops, bytes_accessed=4 * inverse_tiles.size, transcendentals=0
        ),
    )(structure, block_slot, inverse_tiles, panel_blocks, diag_inverse)


def solution(mesh):
    line, wide = grid_of(mesh)
    in_specs = (
        P(("fields", "prow"), "pcol", None, None),
        P("fields", "prow", None, "pcol"),
        P("fields", "pcol"),
        P("fields", None),
        P("fields"),
    )
    out_specs = (P("fields", "prow", None, "pcol"), P("fields", "pcol"))
    return jax.shard_map(
        functools.partial(per_device, line, wide),
        mesh=mesh, in_specs=in_specs, out_specs=out_specs, check_vma=False,
    )
```
